768 devices in a mesh: dp: 32 (over y, x), expert: 12 (over z), tensor: 2 (over core).
Axes of the slice: x: 4, y: 8, z: 12, core: 2. Of those that a mesh axis runs over, the one named last changes fastest.
Arguments:
- tokens: bfloat16 [98304, 4096], P(('dp', 'expert'), 'tensor'), may hold values from -6 to 6
- cotangent: bfloat16 [98304, 4096], P(('dp', 'expert'), 'tensor'), may hold values from -0.099609375 to 0.099609375
- latent_down: bfloat16 [4096, 1024], P('tensor'), may hold values from -0.09375 to 0.09375
- latent_up: bfloat16 [1024, 4096], P(None, 'tensor'), may hold values from -0.1875 to 0.1875
- expert_up: bfloat16 [24, 1024, 512], P(('expert', 'tensor')), may hold values from -0.1875 to 0.1875
- expert_down: bfloat16 [24, 512, 1024], P(('expert', 'tensor')), may hold values from -0.25 to 0.25
- routes: int32 [98304, 2], P(('dp', 'expert', 'tensor')), may hold values from 0 to 23, all different within a row; in each aligned block of 128 rows (0 to 127, 128 to 255, ...) at most 16 rows name the same one
- combine: float32 [98304, 2], P(('dp', 'expert', 'tensor')), may hold values from 0.2 to 1
Outputs:
- grad_up: float32 [24, 1024, 512], P(('expert', 'tensor'), 'dp')
- grad_down: float32 [24, 512, 1024], P(('expert', 'tensor'), 'dp')
The draws below stay inside these ranges and needn't reach their ends.
Inputs may be any that keep to these rules, and one draw needn't show every extreme that they name: `routes`: each token names 2 different experts. The 128 tokens of one device name no expert in more than 16 slots, and in every draw some device names some expert in exactly 16 slots.
All inputs are finite; a program needn't handle non-finite values.
Results may differ from the reference program's by a relative error of at most 0.025.
Values may be sent and summed in bfloat16 or wider, within the bound.
A program may use at most 64 MiB of HBM per device.

```python
import math
import jax
import jax.numpy as jnp
import numpy as np
from jax import lax

D = 4096
L = 1024
H = 512
TOP = 2
TOK_DEV = 128
TOKENS = 98304
EXPERTS = 24
CAP = 16
N_DP = 32
N_TENSOR = 2


def block_scale(own_key, extent, cuts, least, high):
    factor_of = 1.0
    for dim, parts in cuts:
        heights = jax.random.uniform(jax.random.fold_in(jax.random.fold_in(own_key, 6), dim), (parts,), jnp.float32, least / len(cuts), high / len(cuts))
        factor_of = factor_of * jnp.repeat(jnp.exp(heights), extent[dim] // parts).reshape((-1,) + (1,) * (len(extent) - 1 - dim))
    return factor_of


def routed_block(key, own, number, rows, number_of, top, limit, skew):
    sequence = jax.random.permutation(key, number_of)
    crowded, usual = load_shares(number_of, rows * top, limit, skew, True), load_shares(number_of, rows * top, limit, skew, False)
    places = jnp.arange(number_of)

    def named(lengths, offset_by):
        used = int((lengths > 0).sum())
        fixed = max(1, used // 4)
        moved = fixed + (places - fixed + offset_by * (used - fixed)) % max(1, number_of - fixed)
        return jnp.zeros((number_of,), jnp.int32).at[sequence[jnp.where(places < fixed, places, moved)]].set(jnp.asarray(lengths, jnp.int32))

    lengths = jnp.where(number % 4 == 0, named(crowded, number // 4), named(usual, number - number // 4 - 1))
    mixed = jax.random.permutation(jax.random.fold_in(own, 3), number_of)
    source_of, sink = mixed[0:number_of // 2 * 2:2], mixed[1:number_of // 2 * 2:2]
    margin = jnp.minimum(lengths[source_of] - 1, limit - lengths[sink]) // 2
    margin = jnp.where((source_of == sequence[0]) | (sink == sequence[0]) | (lengths[sink] == 0), 0, jnp.maximum(margin, 0))
    moved = jax.random.randint(jax.random.fold_in(own, 4), (number_of // 2,), 0, 1 << 20) % (margin + 1)
    lengths = lengths.at[source_of].add(-moved).at[sink].add(moved)
    items = jnp.searchsorted(jnp.cumsum(lengths), jnp.arange(rows * top), side="right").astype(jnp.int32)
    table = items.reshape(top, rows).T
    table = table[jax.random.permutation(jax.random.fold_in(own, 1), rows)]
    offset_by = jax.random.randint(jax.random.fold_in(own, 2), (rows, 1), 0, top)
    return jnp.take_along_axis(table, (jnp.arange(top)[None, :] + offset_by) % top, axis=1)


def load_shares(amount, total, reach, skew, full):
    loads = [(1 << 20) // math.isqrt(grade ** skew) + 1 for grade in range(1, amount + 1)]
    largest = reach if full else min(reach, max(-(-total // amount), total * loads[0] // sum(loads)))
    least = 1 if total - largest >= amount - 1 else 0
    given, surplus = [largest] + [least] * (amount - 1), total - largest - least * (amount - 1)
    while surplus > 0:
        candidates = [i for i in range(1, amount) if given[i] < largest] or [i for i in range(1, amount) if given[i] < reach]
        mass, budget = sum([loads[i] for i in candidates]), surplus
        for i in candidates:
            extra = min(reach - given[i], max(1, budget * loads[i] // mass), surplus)
            given[i] = given[i] + extra
            surplus = surplus - extra
    return np.array(given)


def bell_draw(own_key, shape, scale, limit, pieces=(), kind=jnp.bfloat16):
    array = scale * jax.random.normal(own_key, shape, jnp.float32)
    if pieces:
        array = array * block_scale(own_key, shape, pieces, -0.22, 0.18)
    return jnp.clip(array, -limit, limit).astype(kind)


def setup_inputs(seed: int = 0) -> dict:
    key_of = jax.random.split(jax.random.key(seed), 9)
    tokens = bell_draw(key_of[0], (TOKENS, D), 1.0, 6.0, ((0, 384), (1, 2)))
    cotangent = bell_draw(key_of[1], (TOKENS, D), 0.015625, 0.099609375, ((0, 384), (1, 2)))
    latent_down = bell_draw(key_of[2], (D, L), D ** -0.5, 0.09375, ((0, 2),))
    latent_up = bell_draw(key_of[3], (L, D), L ** -0.5, 0.1875, ((1, 2),))
    expert_up = bell_draw(key_of[4], (EXPERTS, L, H), L ** -0.5, 0.1875, ((0, 24),))
    expert_down = bell_draw(key_of[5], (EXPERTS, H, L), H ** -0.5, 0.25, ((0, 24),))
    routes_keys = jax.random.split(jax.random.fold_in(key_of[6], 1), TOKENS // TOK_DEV)
    routes_turns = jax.random.permutation(jax.random.fold_in(key_of[6], 3), TOKENS // TOK_DEV)
    routes = jax.vmap(lambda own, number: routed_block(jax.random.fold_in(key_of[6], 2), own, number, TOK_DEV, EXPERTS, TOP, CAP, 2))(routes_keys, routes_turns).reshape((TOKENS, TOP))
    combine = jnp.clip(0.2 + 0.8 * jax.random.uniform(key_of[7], (TOKENS, TOP), jnp.float32) ** block_scale(key_of[7], (TOKENS, TOP), ((0, 768),), -0.2, 0.2), 0.2, 1.0)
    return dict(tokens=tokens, cotangent=cotangent, latent_down=latent_down, latent_up=latent_up, expert_up=expert_up, expert_down=expert_down, routes=routes, combine=combine)


def via_bf16(value):
    return lax.optimization_barrier(value.astype(jnp.bfloat16)).astype(jnp.float32)


def reference(tokens, cotangent, latent_down, latent_up, expert_up, expert_down, routes, combine):
    range_width = D // N_TENSOR
    forward_sum = jnp.zeros((TOKENS, L), jnp.float32)
    backward_sum = jnp.zeros((TOKENS, L), jnp.float32)
    for tensor_rank in range(N_TENSOR):
        first_col = tensor_rank * range_width
        last_col = first_col + range_width
        partial_value = jnp.dot(tokens[:, first_col:last_col], latent_down[first_col:last_col], preferred_element_type=jnp.float32)
        forward_sum = forward_sum + via_bf16(partial_value)
        partial_back = lax.dot_general(cotangent[:, first_col:last_col], latent_up[:, first_col:last_col], (((1,), (1,)), ((), ())), preferred_element_type=jnp.float32)
        backward_sum = backward_sum + via_bf16(partial_back)
    latent = forward_sum.astype(jnp.bfloat16)
    slot_grad = (combine[:, :, None] * backward_sum[:, None, :]).astype(jnp.bfloat16)
    device_count = TOKENS // TOK_DEV
    slots_dev = TOK_DEV * TOP
    chosen = routes.reshape(device_count, slots_dev).astype(jnp.int32)
    onehot = (chosen[:, :, None] == jnp.arange(EXPERTS, dtype=jnp.int32)[None, None, :]).astype(jnp.int32)
    slot_rank = jnp.sum(onehot * (jnp.cumsum(onehot, axis=1) - 1), axis=2).astype(jnp.int32)
    slot_ids = jnp.arange(TOKENS * TOP, dtype=jnp.int32).reshape(device_count, slots_dev)
    device_ids = jnp.broadcast_to(jnp.arange(device_count, dtype=jnp.int32)[:, None], (device_count, slots_dev))
    table = jnp.full((EXPERTS, device_count, CAP), TOKENS * TOP, jnp.int32)
    table = table.at[chosen, device_ids, slot_rank].set(slot_ids)
    latent_ext = jnp.concatenate([latent, jnp.zeros((1, L), jnp.bfloat16)], axis=0)
    grad_ext = jnp.concatenate([slot_grad.reshape(TOKENS * TOP, L), jnp.zeros((1, L), jnp.bfloat16)], axis=0)
    highest = lax.Precision.HIGHEST

    def one_expert(packed):
        picked, weight_up, weight_down = packed
        picked = picked.reshape(N_DP, -1)
        lat_rows = latent_ext[picked // TOP].astype(jnp.float32)
        grad_rows = grad_ext[picked].astype(jnp.float32)
        pre = jnp.einsum('dml,lh->dmh', lat_rows, weight_up.astype(jnp.float32), precision=highest)
        positive = jnp.maximum(pre, 0.0)
        act = (positive * positive).astype(jnp.bfloat16).astype(jnp.float32)
        part_down = jnp.einsum('dmh,dml->dhl', act, grad_rows, precision=highest)
        hidden_grad = jnp.einsum('dml,hl->dmh', grad_rows, weight_down.astype(jnp.float32), precision=highest)
        pre_grad = (hidden_grad * 2.0 * positive).astype(jnp.bfloat16).astype(jnp.float32)
        part_up = jnp.einsum('dml,dmh->dlh', lat_rows, pre_grad, precision=highest)
        total_up = jnp.sum(via_bf16(part_up), axis=0)
        total_down = jnp.sum(via_bf16(part_down), axis=0)
        return total_up, total_down

    grad_up, grad_down = lax.map(one_expert, (table, expert_up, expert_down))
    return grad_up, grad_down
```

```python
import functools

import jax
import jax.numpy as jnp
from jax import lax
from jax.experimental import pallas as pl
from jax.experimental.pallas import tpu as pltpu
from jax.sharding import PartitionSpec as P

F32 = jnp.float32
BF16 = jnp.bfloat16
MESH = pl.DeviceIdType.MESH
NY, NX = 8, 4


def remote(src, dst, send_sem, recv_sem, device):
    return pltpu.make_async_remote_copy(
        src_ref=src,
        dst_ref=dst,
        send_sem=send_sem,
        recv_sem=recv_sem,
        device_id=device,
        device_id_type=MESH,
    )


def dot(a, b, dims=((1,), (0,))):
    return lax.dot_general(a, b, (dims, ((), ())), preferred_element_type=F32)


class RingSum:
    def __init__(self, chunk, land, send_sem, recv_sem, me, n, device):
        self.chunk, self.land = chunk, land
        self.send_sem, self.recv_sem = send_sem, recv_sem
        self.me, self.n, self.half, self.device = me, n, n // 2, device
        self.m = chunk.shape[1]
        self.sent = []

    def part(self, way):
        h = self.m // 2
        return pl.ds(0, h) if way == 0 else pl.ds(h, h)

    def owner(self, way, distance):
        if way == 0:
            return lax.rem(self.me + distance, self.n)
        return lax.rem(self.me + self.n - distance, self.n)

    def copy(self, way, step):
        src = self.chunk.at[self.owner(way, self.half - step)]
        if step == 0:
            src = src.at[self.part(way)]
            dst = self.land.at[way, 0, self.part(way)]
        else:
            dst = self.land.at[way, step]
        return remote(
            src,
            dst,
            self.send_sem.at[way, step],
            self.recv_sem.at[way, step],
            self.device(self.owner(way, 1)),
        )

    def start(self, step):
        for way in (0, 1):
            if step > 0:
                self.copy(way, step - 1).wait_recv()
                target = self.owner(way, self.half - step)
                piece = self.part(way) if step == 1 else pl.ds(0, self.m)
                total = self.chunk[target, piece].astype(F32) + self.land[
                    way, step - 1, piece
                ].astype(F32)
                self.chunk[target, piece] = total.astype(BF16)
            copy = self.copy(way, step)
            copy.start()
            self.sent.append(copy)

    def finish(self):
        step = self.half - 1
        for way in (0, 1):
            self.copy(way, step).wait_recv()
        own = self.chunk[self.me].astype(F32)
        if self.half == 1:
            return own + self.last_halves()
        return own + self.land[0, step].astype(F32) + self.land[1, step].astype(F32)

    def last_halves(self):
        h = self.m // 2
        return jnp.concatenate([self.land[0, 0, :h], self.land[1, 0, h:]], axis=0).astype(F32)


def layer(
    ny, nx, nz, cap,
    tok_hbm, cot_hbm, down_hbm, up_hbm, wup_hbm, wdn_hbm, routes_ref, combine_ref,
    gup_ref, gdn_ref,
    tok, cot, down, up, wup, wdn, load_sem,
    part_f, part_b, got_f, got_b, swap_send, swap_recv,
    out_lat, out_grad, in_lat, in_grad, a2a_send, a2a_recv, own_sem,
    act_ref, pre_grad_ref,
    chunk_a, chunk_b, land_a, land_b, ring_a_send, ring_a_recv, ring_b_send, ring_b_recv,
    next_a, next_b, got_a, got_b2, dir_a_send, dir_a_recv, dir_b_send, dir_b_recv,
):
    group = lax.axis_index("dp")
    z = lax.axis_index("expert")
    core = lax.axis_index("tensor")
    other = 1 - core
    y, x = group // nx, lax.rem(group, nx)
    tok_dev = routes_ref.shape[1]
    width = down.shape[1]
    experts = 2 * nz

    def at_x(xx):
        return {"dp": y * nx + xx}

    def at_y(yy):
        return {"dp": yy * nx + x}

    loads = [
        pltpu.make_async_copy(src, dst, load_sem.at[i])
        for i, (src, dst) in enumerate(
            [(tok_hbm, tok), (down_hbm, down), (cot_hbm, cot), (up_hbm, up), (wup_hbm.at[0], wup), (wdn_hbm.at[0], wdn)]
        )
    ]
    for load in loads:
        load.start()

    barrier = pltpu.get_barrier_semaphore()

    def greet(device):
        pl.semaphore_signal(barrier, inc=1, device_id=device, device_id_type=MESH)

    greet({"tensor": other})
    for k in range(1, nz):
        for cc in range(2):
            greet({"expert": lax.rem(z + k, nz), "tensor": cc})
    for k in range(1, nx):
        greet(at_x(lax.rem(x + k, nx)))
    for k in range(1, ny):
        greet(at_y(lax.rem(y + k, ny)))

    step = min(256, width)
    loads[0].wait()
    loads[1].wait()
    for j in range(0, width, step):
        part_f[:, j : j + step] = dot(tok[...], down[:, j : j + step]).astype(BF16)
    pl.semaphore_wait(barrier, 1 + 2 * (nz - 1) + (nx - 1) + (ny - 1))
    theirs = pl.ds(pl.multiple_of(other * tok_dev, tok_dev), tok_dev)
    mine = pl.ds(pl.multiple_of(core * tok_dev, tok_dev), tok_dev)
    swap_f = remote(part_f.at[theirs], got_f, swap_send.at[0], swap_recv.at[0], {"tensor": other})
    swap_f.start()
    loads[2].wait()
    loads[3].wait()
    for j in range(0, width, step):
        part_b[:, j : j + step] = dot(cot[...], up[j : j + step, :], ((1,), (1,))).astype(BF16)
    swap_b = remote(part_b.at[theirs], got_b, swap_send.at[1], swap_recv.at[1], {"tensor": other})
    swap_b.start()

    before = (
        lax.broadcasted_iota(jnp.int32, (tok_dev, tok_dev), 0)
        < lax.broadcasted_iota(jnp.int32, (tok_dev, tok_dev), 1)
    ).astype(BF16)
    expert_id = lax.broadcasted_iota(jnp.int32, (experts, tok_dev), 0)
    slot_id = lax.broadcasted_iota(jnp.int32, (experts * cap, tok_dev), 0)
    taken = jnp.zeros((experts, 1), F32)
    table = jnp.zeros((experts * cap, tok_dev), F32)
    weight = jnp.zeros((experts * cap, 1), F32)
    for k in range(routes_ref.shape[0]):
        chosen = routes_ref[k : k + 1, :]
        named = (expert_id == chosen).astype(F32)
        count = dot(named.astype(BF16), before) + taken
        rank = jnp.sum(named * count, axis=0, keepdims=True)
        taken = taken + jnp.sum(named, axis=1, keepdims=True)
        here = slot_id == chosen * cap + rank.astype(jnp.int32)
        table = table + here.astype(F32)
        weight = weight + jnp.sum(
            jnp.where(here, combine_ref[k : k + 1, :], 0.0), axis=1, keepdims=True
        )
    table = table.astype(BF16)

    order = sorted(range(1, nz), key=lambda k: -min(k, nz - k))
    sent = []

    def dispatch(which, outgoing, incoming):
        for k in order:
            zz = lax.rem(z + k, nz)
            for cc in range(2):
                copy = remote(
                    outgoing.at[2 * zz + cc],
                    incoming.at[2 * k + core],
                    a2a_send.at[which, 2 * k + cc],
                    a2a_recv.at[which, 2 * k + core],
                    {"expert": zz, "tensor": cc},
                )
                copy.start()
                sent.append(copy)
        copy = remote(
            outgoing.at[2 * z + other],
            incoming.at[core],
            a2a_send.at[which, other],
            a2a_recv.at[which, core],
            {"tensor": other},
        )
        copy.start()
        sent.append(copy)
        own = pltpu.make_async_copy(
            outgoing.at[2 * z + core], incoming.at[core], own_sem.at[which]
        )
        own.start()
        return own

    def collect(which, incoming, own):
        for k in reversed(order):
            for cc in range(2):
                remote(
                    incoming.at[2 * k + cc],
                    incoming.at[2 * k + cc],
                    a2a_send.at[which, 2 * k + cc],
                    a2a_recv.at[which, 2 * k + cc],
                    {"expert": lax.rem(z + k, nz), "tensor": cc},
                ).wait_recv()
        remote(
            incoming.at[other],
            incoming.at[other],
            a2a_send.at[which, other],
            a2a_recv.at[which, other],
            {"tensor": other},
        ).wait_recv()
        own.wait()

    swap_f.wait_recv()
    lat = (part_f[mine].astype(F32) + got_f[...].astype(F32)).astype(BF16)
    out_lat[...] = dot(table, lat).astype(BF16).reshape(out_lat.shape)
    own_lat = dispatch(0, out_lat, in_lat)
    swap_b.wait_recv()
    back = dot(table, part_b[mine]) + dot(table, got_b[...])
    out_grad[...] = (weight * back).astype(BF16).reshape(out_grad.shape)
    own_grad = dispatch(1, out_grad, in_grad)

    loads[4].wait()
    loads[5].wait()
    collect(0, in_lat, own_lat)
    lat_rows = in_lat[...].reshape(-1, width)
    positive = jnp.maximum(dot(lat_rows, wup[...]), 0.0)
    act_ref[...] = (positive * positive).astype(BF16)
    collect(1, in_grad, own_grad)
    grad_rows = in_grad[...].reshape(-1, width)
    hidden_grad = dot(grad_rows, wdn[...], ((1,), (1,)))
    pre_grad_ref[...] = (hidden_grad * 2.0 * positive).astype(BF16)

    rows = chunk_a.shape[2]
    for j in range(0, width, step):
        piece = dot(act_ref[...], grad_rows[:, j : j + step], ((0,), (0,)))
        piece = piece.astype(BF16).reshape(ny, nx, rows, step)
        for xx in range(nx):
            chunk_a[xx, :, :, j : j + step] = piece[:, xx]
    ring_a = RingSum(chunk_a, land_a, ring_a_send, ring_a_recv, x, nx, at_x)
    ring_b = RingSum(chunk_b, land_b, ring_b_send, ring_b_recv, y, ny, at_y)
    ring_a.start(0)
    hidden = wup.shape[1]
    step = min(step, hidden)
    for j in range(0, hidden, step):
        piece = dot(lat_rows, pre_grad_ref[:, j : j + step], ((0,), (0,)))
        piece = piece.astype(BF16).reshape(ny, nx, 2, rows, step)
        for half in range(2):
            chunk_b[:, :, :, half * hidden + j : half * hidden + j + step] = piece[:, :, half]
    ring_b.start(0)
    ring_a.start(1)
    ring_b.start(1)
    ring_b.start(2)
    sum_a = ring_a.finish()
    next_a[...] = sum_a.astype(BF16)

    def spread(source, land, send_sem, recv_sem, me, n, device):
        copies = []
        for k in range(1, n):
            target = lax.rem(me + k, n)
            copy = remote(source.at[target], land.at[k], send_sem.at[k], recv_sem.at[k], device(target))
            copy.start()
            copies.append(copy)
        return copies

    def total(source, land, copies, me):
        out = source[me].astype(F32)
        for k, copy in enumerate(copies, 1):
            copy.wait_recv()
            out = out + land[k].astype(F32)
        return out

    spread_a = spread(next_a, got_a, dir_a_send, dir_a_recv, y, ny, at_y)
    ring_b.start(3)
    next_b[...] = ring_b.finish().astype(BF16)
    spread_b = spread(next_b, got_b2, dir_b_send, dir_b_recv, x, nx, at_x)
    gdn_ref[0] = total(next_a, got_a, spread_a, y)
    sum_b = total(next_b, got_b2, spread_b, x)
    gup_ref[0, 0:rows, :] = sum_b[:, :hidden]
    gup_ref[0, rows : 2 * rows, :] = sum_b[:, hidden:]

    for copy in [swap_f, swap_b] + sent + ring_a.sent + ring_b.sent + spread_a + spread_b:
        copy.wait_send()


def shards(ny, nx, tokens, cotangent, latent_down, latent_up, expert_up, expert_down, routes, combine):
    nz = lax.axis_size("expert")
    tok_dev, top = routes.shape
    width, hidden = expert_up.shape[1:]
    experts = 2 * nz
    cap = max(2, 3 * tok_dev * top // (2 * experts))
    rows = hidden // (ny * nx)
    assert width == 2 * hidden

    def sems(*shape):
        return pltpu.SemaphoreType.DMA(shape)

    vmem = pltpu.VMEM
    any_spec = pl.BlockSpec(memory_space=pl.ANY)
    vmem_spec = pl.BlockSpec(memory_space=pltpu.VMEM)
    return pl.pallas_call(
        functools.partial(layer, ny, nx, nz, cap),
        out_shape=(
            jax.ShapeDtypeStruct((1, width // (ny * nx), hidden), F32),
            jax.ShapeDtypeStruct((1, rows, width), F32),
        ),
        in_specs=[any_spec] * 6 + [vmem_spec] * 2,
        out_specs=(vmem_spec, vmem_spec),
        scratch_shapes=[
            vmem(tokens.shape, BF16), vmem(cotangent.shape, BF16),
            vmem(latent_down.shape, BF16), vmem(latent_up.shape, BF16),
            vmem((width, hidden), BF16), vmem((hidden, width), BF16), sems(6),
            vmem((2 * tok_dev, width), BF16), vmem((2 * tok_dev, width), BF16),
            vmem((tok_dev, width), BF16), vmem((tok_dev, width), BF16), sems(2), sems(2),
            vmem((experts, cap, width), BF16), vmem((experts, cap, width), BF16),
            vmem((experts, cap, width), BF16), vmem((experts, cap, width), BF16),
            sems(2, experts), sems(2, experts), sems(2),
            vmem((experts * cap, hidden), BF16), vmem((experts * cap, hidden), BF16),
            vmem((nx, ny, rows, width), BF16), vmem((ny, nx, rows, width), BF16),
            vmem((2, nx // 2, ny, rows, width), BF16), vmem((2, ny // 2, nx, rows, width), BF16),
            sems(2, nx // 2), sems(2, nx // 2), sems(2, ny // 2), sems(2, ny // 2),
            vmem((ny, rows, width), BF16), vmem((nx, rows, width), BF16),
            vmem((ny, rows, width), BF16), vmem((nx, rows, width), BF16),
            sems(ny), sems(ny), sems(nx), sems(nx),
        ],
        compiler_params=pltpu.CompilerParams(
            collective_id=0, has_side_effects=True, vmem_limit_bytes=56 * 1024 * 1024
        ),
        cost_estimate=pl.CostEstimate(flops=4 * 10**9, bytes_accessed=13 * 10**6, transcendentals=0),
    )(tokens, cotangent, latent_down, latent_up, expert_up, expert_down, routes.T, combine.T)


def solution(mesh):
    return jax.shard_map(
        functools.partial(shards, NY, NX),
        mesh=mesh,
        in_specs=(
            P(("dp", "expert"), "tensor"),
            P(("dp", "expert"), "tensor"),
            P("tensor", None),
            P(None, "tensor"),
            P(("expert", "tensor"), None, None),
            P(("expert", "tensor"), None, None),
            P(("dp", "expert", "tensor"), None),
            P(("dp", "expert", "tensor"), None),
        ),
        out_specs=(P(("expert", "tensor"), "dp", None), P(("expert", "tensor"), "dp", None)),
        check_vma=False,
    )
```

```python
import functools

import jax
import jax.numpy as jnp
from jax import lax
from jax.experimental import pallas as pl
from jax.experimental.pallas import tpu as pltpu
from jax.sharding import PartitionSpec as P

F32 = jnp.float32
BF16 = jnp.bfloat16
MESH = pl.DeviceIdType.MESH
NY, NX = 8, 4


def remote(src, dst, send_sem, recv_sem, device):
    return pltpu.make_async_remote_copy(
        src_ref=src,
        dst_ref=dst,
        send_sem=send_sem,
        recv_sem=recv_sem,
        device_id=device,
        device_id_type=MESH,
    )


def dot(a, b, dims=((1,), (0,))):
    return lax.dot_general(a, b, (dims, ((), ())), preferred_element_type=F32)


class Direct:
    def __init__(self, source, landing, sems, me, n, device):
        send_sem, recv_sem = sems
        self.sent, self.recv = [], []
        for k in range(1, n):
            target = lax.rem(me + k, n)
            sender = lax.rem(me + n - k, n)
            copy = remote(
                source(target), landing(me, k), send_sem.at[k], recv_sem.at[k], device(target)
            )
            copy.start()
            self.sent.append(copy)
            here = landing(sender, k)
            self.recv.append(remote(here, here, send_sem.at[k], recv_sem.at[k], device(target)))

    def wait(self):
        for copy in self.recv:
            copy.wait_recv()


class Ring:
    def __init__(self, me, n, device):
        self.me, self.n, self.device = me, n, device


class TwoStepSum:
    def __init__(self, refs, first, second):
        self.chunk, self.land, self.next, self.got, send1, recv1, send2, recv2 = refs
        self.first, self.second = first, second
        self.sems1, self.sems2 = (send1, recv1), (send2, recv2)

    def start(self):
        r = self.first
        self.step1 = Direct(
            lambda t: self.chunk.at[t], lambda s, k: self.land.at[k], self.sems1, r.me, r.n, r.device
        )

    def turn(self):
        self.step1.wait()
        total = self.chunk[self.first.me].astype(F32)
        for k in range(1, self.first.n):
            total = total + self.land[k].astype(F32)
        self.next[...] = total.astype(BF16)
        r = self.second
        self.step2 = Direct(
            lambda t: self.next.at[t], lambda s, k: self.got.at[k], self.sems2, r.me, r.n, r.device
        )

    def total(self):
        self.step2.wait()
        total = self.next[self.second.me].astype(F32)
        for k in range(1, self.second.n):
            total = total + self.got[k].astype(F32)
        return total

    def sent(self):
        return self.step1.sent + self.step2.sent


class PlaneSum:
    def __init__(self, refs, xs, ys):
        n = len(refs) // 3
        self.down = TwoStepSum(refs[:n], xs, ys)
        self.up0 = TwoStepSum(refs[n : 2 * n], xs, ys)
        self.up1 = TwoStepSum(refs[2 * n :], ys, xs)

    def sent(self):
        return self.down.sent() + self.up0.sent() + self.up1.sent()


def layer(
    ny, nx, nz, cap,
    tok_hbm, cot_hbm, down_hbm, up_hbm, wup_hbm, wdn_hbm, routes_ref, combine_ref,
    gup_ref, gdn_ref,
    tok, cot, down, up, wup, wdn, load_sem,
    part_f, part_b, got_f, got_b, swap_send, swap_recv,
    out_lat, out_grad, in_lat, in_grad, a2a_send, a2a_recv, own_sem,
    wup2, wdn2, slice_send, slice_recv,
    act_ref, pre_grad_ref, far_out, far_in, far_send, far_recv,
    *more,
):
    group = lax.axis_index("dp")
    z = lax.axis_index("expert")
    core = lax.axis_index("tensor")
    other = 1 - core
    y, x = group // nx, lax.rem(group, nx)
    tok_dev = routes_ref.shape[1]
    width, hidden = wup.shape
    experts = 2 * nz
    far = nz // 2
    reach = nz // 4
    far_z = lax.rem(z + far, nz)

    xs = Ring(x, nx, lambda xx: {"dp": y * nx + xx})
    ys = Ring(y, ny, lambda yy: {"dp": yy * nx + x})

    def plane(j):
        return lax.rem(z + j + nz, nz)

    loads = [
        pltpu.make_async_copy(src, dst, load_sem.at[i])
        for i, (src, dst) in enumerate(
            [(tok_hbm, tok), (down_hbm, down), (cot_hbm, cot), (up_hbm, up), (wup_hbm.at[0], wup), (wdn_hbm.at[0], wdn)]
        )
    ]
    for load in loads:
        load.start()

    barrier = pltpu.get_barrier_semaphore()
    greeted = []

    def greet(device):
        greeted.append(device)
        pl.semaphore_signal(barrier, inc=1, device_id=device, device_id_type=MESH)

    greet({"tensor": other})
    for j in range(1, nz):
        for cc in range(2):
            greet({"expert": plane(j), "tensor": cc})
    for k in range(1, nx):
        greet(xs.device(lax.rem(x + k, nx)))
    for k in range(1, ny):
        greet(ys.device(lax.rem(y + k, ny)))

    step = min(256, width)
    loads[0].wait()
    loads[1].wait()
    for j in range(0, width, step):
        part_f[:, j : j + step] = dot(tok[...], down[:, j : j + step]).astype(BF16)
    pl.semaphore_wait(barrier, len(greeted))
    theirs = pl.ds(pl.multiple_of(other * tok_dev, tok_dev), tok_dev)
    mine = pl.ds(pl.multiple_of(core * tok_dev, tok_dev), tok_dev)
    swap_f = remote(part_f.at[theirs], got_f, swap_send.at[0], swap_recv.at[0], {"tensor": other})
    swap_f.start()

    up_rows, dn_rows = wup2.shape[2], wdn2.shape[2]
    slices = [
        remote(
            wup_hbm.at[0, pl.ds(pl.multiple_of(group * up_rows, up_rows), up_rows)],
            wup2.at[y, x], slice_send.at[0], slice_recv.at[0], {"expert": far_z},
        ),
        remote(
            wdn_hbm.at[0, pl.ds(pl.multiple_of(group * dn_rows, dn_rows), dn_rows)],
            wdn2.at[y, x], slice_send.at[1], slice_recv.at[1], {"expert": far_z},
        ),
    ]

    @pl.when(core == 0)
    def _():
        for copy in slices:
            copy.start()

    loads[2].wait()
    loads[3].wait()
    for j in range(0, width, step):
        part_b[:, j : j + step] = dot(cot[...], up[j : j + step, :], ((1,), (1,))).astype(BF16)
    swap_b = remote(part_b.at[theirs], got_b, swap_send.at[1], swap_recv.at[1], {"tensor": other})
    swap_b.start()

    before = (
        lax.broadcasted_iota(jnp.int32, (tok_dev, tok_dev), 0)
        < lax.broadcasted_iota(jnp.int32, (tok_dev, tok_dev), 1)
    ).astype(BF16)
    expert_id = lax.broadcasted_iota(jnp.int32, (experts, tok_dev), 0)
    slot_id = lax.broadcasted_iota(jnp.int32, (experts * cap, tok_dev), 0)
    taken = jnp.zeros((experts, 1), F32)
    table = jnp.zeros((experts * cap, tok_dev), F32)
    weight = jnp.zeros((experts * cap, 1), F32)
    for k in range(routes_ref.shape[0]):
        chosen = routes_ref[k : k + 1, :]
        named = (expert_id == chosen).astype(F32)
        count = dot(named.astype(BF16), before) + taken
        rank = jnp.sum(named * count, axis=0, keepdims=True)
        taken = taken + jnp.sum(named, axis=1, keepdims=True)
        here = slot_id == chosen * cap + rank.astype(jnp.int32)
        table = table + here.astype(F32)
        weight = weight + jnp.sum(
            jnp.where(here, combine_ref[k : k + 1, :], 0.0), axis=1, keepdims=True
        )
    table = table.astype(BF16)

    second = [(k, k - far) for k in range(nz) if reach < k < nz - reach]
    first = [(k, k if k <= reach else k - nz) for k in range(nz) if k <= reach or k >= nz - reach]
    second_blocks, first_blocks = 2 * len(second), 2 * len(first)

    def places(moves, start):
        low = min(j for _, j in moves)
        return sorted([(k, j, start + 2 * (j - low)) for k, j in moves], key=lambda m: -abs(m[1]))

    second, first = places(second, 0), places(first, second_blocks)
    single = sorted([(k, k, 2 * k) for k in range(nz)], key=lambda m: -min(m[0], nz - m[0]))
    buffers = ((out_lat, in_lat), (out_grad, in_grad))

    def send(which, k, j, base, to, stay):
        outgoing, incoming = buffers[which]
        block = outgoing.at[2 * lax.rem(z + k, nz) + to]
        if stay:
            return pltpu.make_async_copy(block, incoming.at[base + to], own_sem.at[which, 0 if k == 0 else 1])
        return remote(
            block,
            incoming.at[base + core],
            a2a_send.at[which, nz * to + k],
            a2a_recv.at[which, base + core],
            {"tensor": to} if j == 0 else {"expert": plane(j), "tensor": to},
        )

    sent = []

    def dispatch(which, moves, to):
        for k, j, base in moves:
            if j != 0:
                copy = send(which, k, j, base, to, False)
                copy.start()
                sent.append(copy)
                continue

            @pl.when(core == to)
            def _():
                send(which, k, j, base, to, True).start()

            @pl.when(core != to)
            def _():
                send(which, k, j, base, to, False).start()

    def collect(which, moves, me):
        incoming = buffers[which][1]
        for k, j, base in reversed(moves):
            for source in range(2):
                if j == 0 and source == me:
                    send(which, k, j, base, me, True).wait()
                    continue
                here = incoming.at[base + source]
                remote(
                    here, here, a2a_send.at[which, k], a2a_recv.at[which, base + source], {"tensor": other}
                ).wait_recv()

    swap_f.wait_recv()
    lat = (part_f[mine].astype(F32) + got_f[...].astype(F32)).astype(BF16)
    out_lat[...] = dot(table, lat).astype(BF16).reshape(out_lat.shape)
    dispatch(0, first, 0)
    swap_b.wait_recv()
    back = dot(table, part_b[mine]) + dot(table, got_b[...])
    out_grad[...] = (weight * back).astype(BF16).reshape(out_grad.shape)
    dispatch(1, first, 0)
    dispatch(0, second, 0)
    dispatch(1, second, 0)
    dispatch(0, single, 1)
    dispatch(1, single, 1)

    per_sum = len(SUM_PARTS) * 8
    sums = [PlaneSum(more[i * per_sum : (i + 1) * per_sum], xs, ys) for i in range(2)]
    gather = more[2 * per_sum :]

    def expert(moves, me, start, blocks, weight_up, weight_down, summed):
        block = pl.ds(start, blocks)
        rows = pl.ds(start * cap, blocks * cap)
        collect(0, moves, me)
        lat_rows = in_lat[block].reshape(-1, width)
        positive = jnp.maximum(dot(lat_rows, weight_up), 0.0)
        act_ref[rows] = (positive * positive).astype(BF16)
        collect(1, moves, me)
        grad_rows = in_grad[block].reshape(-1, width)
        hidden_grad = dot(grad_rows, weight_down, ((1,), (1,)))
        pre_grad_ref[rows] = (hidden_grad * 2.0 * positive).astype(BF16)
        for j in range(0, width, step):
            piece = dot(act_ref[rows], grad_rows[:, j : j + step], ((0,), (0,)))
            piece = piece.astype(BF16).reshape(ny, nx, dn_rows, step)
            for xx in range(nx):
                summed.down.chunk[xx, :, :, j : j + step] = piece[:, xx]
        summed.down.start()
        cut = min(step, hidden)
        for j in range(0, hidden, cut):
            piece = dot(lat_rows, pre_grad_ref[rows, j : j + cut], ((0,), (0,)))
            piece = piece.astype(BF16).reshape(ny, nx, 2, dn_rows, cut)
            for xx in range(nx):
                summed.up0.chunk[xx, :, :, j : j + cut] = piece[:, xx, 0]
            summed.up1.chunk[:, :, :, j : j + cut] = piece[:, :, 1]
        summed.up1.start()
        summed.up0.start()

    def finish(down_sum, up0_sum, up1_sum):
        gdn_ref[0] = down_sum
        gup_ref[0, 0:dn_rows, :] = up0_sum
        gup_ref[0, dn_rows : 2 * dn_rows, :] = up1_sum

    def sent_within(to, moves):
        for k, j, base in moves:
            if j == 0:
                for which in range(2):
                    send(which, k, j, base, to, False).wait_send()

    @pl.when(core == 0)
    def _():
        up0, up1 = pl.ds(0, dn_rows), pl.ds(dn_rows, dn_rows)
        g = [gather[2 * i : 2 * i + 2] for i in range(6)]
        for copy in slices:
            copy.wait_recv()
        a1 = Direct(lambda t: wdn2.at[y, x], lambda s, k: wdn2.at[s, x], g[0], y, ny, ys.device)
        b1 = Direct(lambda t: wup2.at[y, x, up1], lambda s, k: wup2.at[y, s, up1], g[2], x, nx, xs.device)
        c1 = Direct(lambda t: wup2.at[y, x, up0], lambda s, k: wup2.at[s, x, up0], g[1], y, ny, ys.device)
        b1.wait()
        b2 = Direct(lambda t: wup2.at[y, :, up1], lambda s, k: wup2.at[s, :, up1], g[5], y, ny, ys.device)
        a1.wait()
        a2 = Direct(lambda t: wdn2.at[:, x], lambda s, k: wdn2.at[:, s], g[3], x, nx, xs.device)
        c1.wait()
        c2 = Direct(lambda t: wup2.at[:, x, up0], lambda s, k: wup2.at[:, s, up0], g[4], x, nx, xs.device)

        home, away = sums
        loads[4].wait()
        loads[5].wait()
        expert(first, 0, second_blocks, first_blocks, wup[...], wdn[...], home)
        for part in (a2, b2, c2):
            part.wait()
        expert(
            second, 0, 0, second_blocks,
            wup2[...].reshape(width, hidden), wdn2[...].reshape(hidden, width), away,
        )
        for summed in (home, away):
            summed.down.turn()
            summed.up1.turn()
            summed.up0.turn()
        far_out[0, :, :width] = away.down.total().astype(BF16)
        far_out[0, :, width : width + hidden] = away.up0.total().astype(BF16)
        far_out[0, :, width + hidden :] = away.up1.total().astype(BF16)
        back_home = remote(far_out, far_in, far_send, far_recv, {"expert": far_z})
        back_home.start()
        totals = [home.down.total(), home.up0.total(), home.up1.total()]
        back_home.wait_recv()
        finish(
            totals[0] + far_in[0, :, :width].astype(F32),
            totals[1] + far_in[0, :, width : width + hidden].astype(F32),
            totals[2] + far_in[0, :, width + hidden :].astype(F32),
        )
        sent_within(1, single)
        for copy in slices + [back_home] + home.sent() + away.sent():
            copy.wait_send()
        for part in (a1, b1, c1, a2, b2, c2):
            for copy in part.sent:
                copy.wait_send()

    @pl.when(core == 1)
    def _():
        loads[4].wait()
        loads[5].wait()
        summed = sums[0]
        expert(single, 1, 0, 2 * nz, wup[...], wdn[...], summed)
        summed.down.turn()
        summed.up1.turn()
        summed.up0.turn()
        finish(summed.down.total(), summed.up0.total(), summed.up1.total())
        sent_within(0, first + second)
        for copy in summed.sent():
            copy.wait_send()

    for copy in [swap_f, swap_b] + sent:
        copy.wait_send()


SUM_PARTS = ("down", "up0", "up1")


def shards(ny, nx, tokens, cotangent, latent_down, latent_up, expert_up, expert_down, routes, combine):
    nz = lax.axis_size("expert")
    tok_dev, top = routes.shape
    width, hidden = expert_up.shape[1:]
    experts = 2 * nz
    cap = max(2, 3 * tok_dev * top // (2 * experts))
    rows = hidden // (ny * nx)
    assert width == 2 * hidden

    def sems(*shape):
        return pltpu.SemaphoreType.DMA(shape)

    vmem = pltpu.VMEM
    any_spec = pl.BlockSpec(memory_space=pl.ANY)
    vmem_spec = pl.BlockSpec(memory_space=pltpu.VMEM)

    def two_step(n1, n2, columns):
        return [
            vmem((n1, n2, rows, columns), BF16), vmem((n1, n2, rows, columns), BF16),
            vmem((n2, rows, columns), BF16), vmem((n2, rows, columns), BF16),
            sems(n1), sems(n1), sems(n2), sems(n2),
        ]

    plane_sum = two_step(nx, ny, width) + two_step(nx, ny, hidden) + two_step(ny, nx, hidden)
    gather = [sems(n) for n in (ny, ny, ny, ny, nx, nx, nx, nx, nx, nx, ny, ny)]
    return pl.pallas_call(
        functools.partial(layer, ny, nx, nz, cap),
        out_shape=(
            jax.ShapeDtypeStruct((1, width // (ny * nx), hidden), F32),
            jax.ShapeDtypeStruct((1, rows, width), F32),
        ),
        in_specs=[any_spec] * 6 + [vmem_spec] * 2,
        out_specs=(vmem_spec, vmem_spec),
        scratch_shapes=[
            vmem(tokens.shape, BF16), vmem(cotangent.shape, BF16),
            vmem(latent_down.shape, BF16), vmem(latent_up.shape, BF16),
            vmem((width, hidden), BF16), vmem((hidden, width), BF16), sems(6),
            vmem((2 * tok_dev, width), BF16), vmem((2 * tok_dev, width), BF16),
            vmem((tok_dev, width), BF16), vmem((tok_dev, width), BF16), sems(2), sems(2),
            vmem((experts, cap, width), BF16), vmem((experts, cap, width), BF16),
            vmem((experts, cap, width), BF16), vmem((experts, cap, width), BF16),
            sems(2, experts), sems(2, experts), sems(2, 2),
            vmem((ny, nx, 2 * rows, hidden), BF16), vmem((ny, nx, rows, width), BF16), sems(2), sems(2),
            vmem((experts * cap, hidden), BF16), vmem((experts * cap, hidden), BF16),
            vmem((1, rows, 2 * width), BF16), vmem((1, rows, 2 * width), BF16),
            pltpu.SemaphoreType.DMA, pltpu.SemaphoreType.DMA,
        ]
        + plane_sum
        + plane_sum
        + gather,
        compiler_params=pltpu.CompilerParams(
            collective_id=0, has_side_effects=True, vmem_limit_bytes=56 * 1024 * 1024
        ),
        cost_estimate=pl.CostEstimate(flops=4 * 10**9, bytes_accessed=13 * 10**6, transcendentals=0),
    )(tokens, cotangent, latent_down, latent_up, expert_up, expert_down, routes.T, combine.T)


def solution(mesh):
    return jax.shard_map(
        functools.partial(shards, NY, NX),
        mesh=mesh,
        in_specs=(
            P(("dp", "expert"), "tensor"),
            P(("dp", "expert"), "tensor"),
            P("tensor", None),
            P(None, "tensor"),
            P(("expert", "tensor"), None, None),
            P(("expert", "tensor"), None, None),
            P(("dp", "expert", "tensor"), None),
            P(("dp", "expert", "tensor"), None),
        ),
        out_specs=(P(("expert", "tensor"), "dp", None), P(("expert", "tensor"), "dp", None)),
        check_vma=False,
    )
```

```python
import functools

import jax
import jax.numpy as jnp
from jax import lax
from jax.experimental import pallas as pl
from jax.experimental.pallas import tpu as pltpu
from jax.sharding import PartitionSpec as P

F32 = jnp.float32
BF16 = jnp.bfloat16
MESH = pl.DeviceIdType.MESH
NY, NX = 8, 4


def remote(src, dst, send_sem, recv_sem, device):
    return pltpu.make_async_remote_copy(
        src_ref=src,
        dst_ref=dst,
        send_sem=send_sem,
        recv_sem=recv_sem,
        device_id=device,
        device_id_type=MESH,
    )


def dot(a, b, dims=((1,), (0,))):
    return lax.dot_general(a, b, (dims, ((), ())), preferred_element_type=F32)


class Direct:
    def __init__(self, source, landing, sems, me, n, device):
        send_sem, recv_sem = sems
        self.sent, self.recv = [], []
        for k in range(1, n):
            target = lax.rem(me + k, n)
            sender = lax.rem(me + n - k, n)
            copy = remote(
                source(target), landing(me, k), send_sem.at[k], recv_sem.at[k], device(target)
            )
            copy.start()
            self.sent.append(copy)
            here = landing(sender, k)
            self.recv.append(remote(here, here, send_sem.at[k], recv_sem.at[k], device(target)))

    def wait(self):
        for copy in self.recv:
            copy.wait_recv()


class Ring:
    def __init__(self, me, n, device):
        self.me, self.n, self.device = me, n, device


class TwoStepSum:
    def __init__(self, refs, first, second):
        self.chunk, self.land, self.next, self.got, send1, recv1, send2, recv2 = refs
        self.first, self.second = first, second
        self.sems1, self.sems2 = (send1, recv1), (send2, recv2)

    def start(self):
        r = self.first
        self.step1 = Direct(
            lambda t: self.chunk.at[t], lambda s, k: self.land.at[k], self.sems1, r.me, r.n, r.device
        )

    def turn(self):
        self.step1.wait()
        r = self.second

        def ready(target):
            total = self.chunk[self.first.me, target].astype(F32)
            for k in range(1, self.first.n):
                total = total + self.land[k, target].astype(F32)
            self.next[target] = total.astype(BF16)
            return self.next.at[target]

        self.step2 = Direct(ready, lambda s, k: self.got.at[k], self.sems2, r.me, r.n, r.device)
        ready(r.me)

    def total(self):
        self.step2.wait()
        total = self.next[self.second.me].astype(F32)
        for k in range(1, self.second.n):
            total = total + self.got[k].astype(F32)
        return total

    def sent(self):
        return self.step1.sent + self.step2.sent


class PlaneSum:
    def __init__(self, refs, xs, ys):
        n = len(refs) // 4
        self.down = [TwoStepSum(refs[i * n : (i + 1) * n], xs, ys) for i in (0, 1)]
        self.up0 = TwoStepSum(refs[2 * n : 3 * n], xs, ys)
        self.up1 = TwoStepSum(refs[3 * n :], ys, xs)

    def turn(self):
        for part in self.down + [self.up1, self.up0]:
            part.turn()

    def totals(self):
        return [part.total() for part in self.down + [self.up0, self.up1]]

    def sent(self):
        return self.down[0].sent() + self.down[1].sent() + self.up0.sent() + self.up1.sent()


def layer(
    ny, nx, nz, cap,
    tok_hbm, cot_hbm, down_hbm, up_hbm, wup_hbm, wdn_hbm, routes_ref, combine_ref,
    gup_ref, gdn_ref,
    tok, cot, down, up, wup, wdn, load_sem,
    part_f, part_b, got_f, got_b, swap_send, swap_recv,
    out_lat, out_grad, in_lat, in_grad, a2a_send, a2a_recv, own_sem,
    wup2, wdn2, slice_send, slice_recv,
    act_ref, pre_grad_ref, far_out, far_in, far_send, far_recv,
    *more,
):
    group = lax.axis_index("dp")
    z = lax.axis_index("expert")
    core = lax.axis_index("tensor")
    other = 1 - core
    y, x = group // nx, lax.rem(group, nx)
    tok_dev = routes_ref.shape[1]
    width, hidden = wup.shape
    experts = 2 * nz
    far = nz // 2
    reach = nz // 4
    far_z = lax.rem(z + far, nz)

    xs = Ring(x, nx, lambda xx: {"dp": y * nx + xx})
    ys = Ring(y, ny, lambda yy: {"dp": yy * nx + x})

    def plane(j):
        return lax.rem(z + j + nz, nz)

    loads = [
        pltpu.make_async_copy(src, dst, load_sem.at[i])
        for i, (src, dst) in enumerate(
            [(tok_hbm, tok), (down_hbm, down), (cot_hbm, cot), (up_hbm, up), (wup_hbm.at[0], wup), (wdn_hbm.at[0], wdn)]
        )
    ]
    for load in loads[:2]:
        load.start()

    barrier = pltpu.get_barrier_semaphore()
    greeted = []

    def greet(device):
        greeted.append(device)
        pl.semaphore_signal(barrier, inc=1, device_id=device, device_id_type=MESH)

    greet({"tensor": other})
    for j in range(1, nz):
        for cc in range(2):
            greet({"expert": plane(j), "tensor": cc})
    for k in range(1, nx):
        greet(xs.device(lax.rem(x + k, nx)))
    for k in range(1, ny):
        greet(ys.device(lax.rem(y + k, ny)))

    for load in loads[2:]:
        load.start()

    step = min(256, width)
    loads[0].wait()
    loads[1].wait()
    for j in range(0, width, step):
        part_f[:, j : j + step] = dot(tok[...], down[:, j : j + step]).astype(BF16)
    loads[2].wait()
    loads[3].wait()
    for j in range(0, width, step):
        part_b[:, j : j + step] = dot(cot[...], up[j : j + step, :], ((1,), (1,))).astype(BF16)
    before = (
        lax.broadcasted_iota(jnp.int32, (tok_dev, tok_dev), 0)
        < lax.broadcasted_iota(jnp.int32, (tok_dev, tok_dev), 1)
    ).astype(BF16)
    expert_id = lax.broadcasted_iota(jnp.int32, (experts, tok_dev), 0)
    slot_id = lax.broadcasted_iota(jnp.int32, (experts * cap, tok_dev), 0)
    taken = jnp.zeros((experts, 1), F32)
    table = jnp.zeros((experts * cap, tok_dev), F32)
    weight = jnp.zeros((experts * cap, 1), F32)
    for k in range(routes_ref.shape[0]):
        chosen = routes_ref[k : k + 1, :]
        named = (expert_id == chosen).astype(F32)
        count = dot(named.astype(BF16), before) + taken
        rank = jnp.sum(named * count, axis=0, keepdims=True)
        taken = taken + jnp.sum(named, axis=1, keepdims=True)
        here = slot_id == chosen * cap + rank.astype(jnp.int32)
        table = table + here.astype(F32)
        weight = weight + jnp.sum(
            jnp.where(here, combine_ref[k : k + 1, :], 0.0), axis=1, keepdims=True
        )
    table = table.astype(BF16)

    pl.semaphore_wait(barrier, len(greeted))
    theirs = pl.ds(pl.multiple_of(other * tok_dev, tok_dev), tok_dev)
    mine = pl.ds(pl.multiple_of(core * tok_dev, tok_dev), tok_dev)
    swap_f = remote(part_f.at[theirs], got_f, swap_send.at[0], swap_recv.at[0], {"tensor": other})
    swap_f.start()
    swap_b = remote(part_b.at[theirs], got_b, swap_send.at[1], swap_recv.at[1], {"tensor": other})
    swap_b.start()

    up_rows, dn_rows = wup2.shape[2], wdn2.shape[2]
    slices = [
        remote(
            wup_hbm.at[0, pl.ds(pl.multiple_of(group * up_rows, up_rows), up_rows)],
            wup2.at[y, x], slice_send.at[0], slice_recv.at[0], {"expert": far_z},
        ),
        remote(
            wdn_hbm.at[0, pl.ds(pl.multiple_of(group * dn_rows, dn_rows), dn_rows)],
            wdn2.at[y, x], slice_send.at[1], slice_recv.at[1], {"expert": far_z},
        ),
    ]

    @pl.when(core == 0)
    def _():
        for copy in slices:
            copy.start()

    second = [(k, k - far) for k in range(nz) if reach < k < nz - reach]
    first = [(k, k if k <= reach else k - nz) for k in range(nz) if k <= reach or k >= nz - reach]
    second_blocks, first_blocks = 2 * len(second), 2 * len(first)

    def places(moves, start):
        low = min(j for _, j in moves)
        return sorted([(k, j, start + 2 * (j - low)) for k, j in moves], key=lambda m: -abs(m[1]))

    second, first = places(second, 0), places(first, second_blocks)
    single = sorted([(k, k, 2 * k) for k in range(nz)], key=lambda m: -min(m[0], nz - m[0]))
    buffers = ((out_lat, in_lat), (out_grad, in_grad))

    def send(which, k, j, base, to, stay):
        outgoing, incoming = buffers[which]
        block = outgoing.at[2 * lax.rem(z + k, nz) + to]
        if stay:
            return pltpu.make_async_copy(block, incoming.at[base + to], own_sem.at[which, 0 if k == 0 else 1])
        return remote(
            block,
            incoming.at[base + core],
            a2a_send.at[which, nz * to + k],
            a2a_recv.at[which, base + core],
            {"tensor": to} if j == 0 else {"expert": plane(j), "tensor": to},
        )

    sent = []

    def dispatch(which, moves, to):
        for k, j, base in moves:
            if j != 0:
                copy = send(which, k, j, base, to, False)
                copy.start()
                sent.append(copy)
                continue

            @pl.when(core == to)
            def _():
                send(which, k, j, base, to, True).start()

            @pl.when(core != to)
            def _():
                send(which, k, j, base, to, False).start()

    def collect(which, moves, me):
        incoming = buffers[which][1]
        for k, j, base in reversed(moves):
            for source in range(2):
                if j == 0 and source == me:
                    send(which, k, j, base, me, True).wait()
                    continue
                here = incoming.at[base + source]
                remote(
                    here, here, a2a_send.at[which, k], a2a_recv.at[which, base + source], {"tensor": other}
                ).wait_recv()

    swap_f.wait_recv()
    lat = (part_f[mine].astype(F32) + got_f[...].astype(F32)).astype(BF16)
    out_lat[...] = dot(table, lat).astype(BF16).reshape(out_lat.shape)
    dispatch(0, first, 0)
    swap_b.wait_recv()
    back = dot(table, part_b[mine]) + dot(table, got_b[...])
    out_grad[...] = (weight * back).astype(BF16).reshape(out_grad.shape)
    dispatch(1, first, 0)
    dispatch(0, second, 0)
    dispatch(1, second, 0)
    dispatch(0, single, 1)
    dispatch(1, single, 1)

    per_sum = 4 * 8
    sums = [PlaneSum(more[i * per_sum : (i + 1) * per_sum], xs, ys) for i in range(2)]
    gather = more[2 * per_sum :]

    def expert(moves, me, start, blocks, weight_up, weight_down, summed):
        block = pl.ds(start, blocks)
        rows = pl.ds(start * cap, blocks * cap)
        collect(0, moves, me)
        lat_rows = in_lat[block].reshape(-1, width)
        positive = jnp.maximum(dot(lat_rows, weight_up), 0.0)
        act_ref[rows] = (positive * positive).astype(BF16)
        collect(1, moves, me)
        grad_rows = in_grad[block].reshape(-1, width)
        hidden_grad = dot(grad_rows, weight_down, ((1,), (1,)))
        pre_grad_ref[rows] = (hidden_grad * 2.0 * positive).astype(BF16)
        cut = min(step, hidden)
        for j in range(0, width, cut):
            piece = dot(act_ref[rows], grad_rows[:, j : j + cut], ((0,), (0,)))
            piece = piece.astype(BF16).reshape(ny, nx, dn_rows, cut)
            part, at = summed.down[j // hidden], j % hidden
            for xx in range(nx):
                part.chunk[xx, :, :, at : at + cut] = piece[:, xx]
            if at + cut == hidden:
                part.start()
        for j in range(0, hidden, cut):
            piece = dot(lat_rows, pre_grad_ref[rows, j : j + cut], ((0,), (0,)))
            piece = piece.astype(BF16).reshape(ny, nx, 2, dn_rows, cut)
            for xx in range(nx):
                summed.up0.chunk[xx, :, :, j : j + cut] = piece[:, xx, 0]
            summed.up1.chunk[:, :, :, j : j + cut] = piece[:, :, 1]
        summed.up1.start()
        summed.up0.start()

    def finish(totals):
        for i in range(2):
            gdn_ref[0, :, i * hidden : (i + 1) * hidden] = totals[i]
            gup_ref[0, i * dn_rows : (i + 1) * dn_rows, :] = totals[2 + i]

    def sent_within(to, moves):
        for k, j, base in moves:
            if j == 0:
                for which in range(2):
                    send(which, k, j, base, to, False).wait_send()

    @pl.when(core == 0)
    def _():
        up0, up1 = pl.ds(0, dn_rows), pl.ds(dn_rows, dn_rows)
        g = [gather[2 * i : 2 * i + 2] for i in range(6)]
        for copy in slices:
            copy.wait_recv()
        a1 = Direct(lambda t: wdn2.at[y, x], lambda s, k: wdn2.at[s, x], g[0], y, ny, ys.device)
        b1 = Direct(lambda t: wup2.at[y, x, up1], lambda s, k: wup2.at[y, s, up1], g[2], x, nx, xs.device)
        c1 = Direct(lambda t: wup2.at[y, x, up0], lambda s, k: wup2.at[s, x, up0], g[1], y, ny, ys.device)
        b1.wait()
        b2 = Direct(lambda t: wup2.at[y, :, up1], lambda s, k: wup2.at[s, :, up1], g[5], y, ny, ys.device)
        a1.wait()
        a2 = Direct(lambda t: wdn2.at[:, x], lambda s, k: wdn2.at[:, s], g[3], x, nx, xs.device)
        c1.wait()
        c2 = Direct(lambda t: wup2.at[:, x, up0], lambda s, k: wup2.at[:, s, up0], g[4], x, nx, xs.device)

        home, away = sums
        loads[4].wait()
        loads[5].wait()
        expert(first, 0, second_blocks, first_blocks, wup[...], wdn[...], home)
        for part in (a2, b2, c2):
            part.wait()
        expert(
            second, 0, 0, second_blocks,
            wup2[...].reshape(width, hidden), wdn2[...].reshape(hidden, width), away,
        )
        home.turn()
        away.turn()
        for i, part in enumerate(away.totals()):
            far_out[0, :, i * hidden : (i + 1) * hidden] = part.astype(BF16)
        back_home = remote(far_out, far_in, far_send, far_recv, {"expert": far_z})
        back_home.start()
        totals = home.totals()
        back_home.wait_recv()
        finish([
            part + far_in[0, :, i * hidden : (i + 1) * hidden].astype(F32)
            for i, part in enumerate(totals)
        ])
        sent_within(1, single)
        for copy in slices + [back_home] + home.sent() + away.sent():
            copy.wait_send()
        for part in (a1, b1, c1, a2, b2, c2):
            for copy in part.sent:
                copy.wait_send()

    @pl.when(core == 1)
    def _():
        loads[4].wait()
        loads[5].wait()
        summed = sums[0]
        expert(single, 1, 0, 2 * nz, wup[...], wdn[...], summed)
        summed.turn()
        finish(summed.totals())
        sent_within(0, first + second)
        for copy in summed.sent():
            copy.wait_send()

    for copy in [swap_f, swap_b] + sent:
        copy.wait_send()


def shards(ny, nx, tokens, cotangent, latent_down, latent_up, expert_up, expert_down, routes, combine):
    nz = lax.axis_size("expert")
    tok_dev, top = routes.shape
    width, hidden = expert_up.shape[1:]
    experts = 2 * nz
    cap = max(2, 3 * tok_dev * top // (2 * experts))
    rows = hidden // (ny * nx)
    assert width == 2 * hidden

    def sems(*shape):
        return pltpu.SemaphoreType.DMA(shape)

    vmem = pltpu.VMEM
    any_spec = pl.BlockSpec(memory_space=pl.ANY)
    vmem_spec = pl.BlockSpec(memory_space=pltpu.VMEM)

    def two_step(n1, n2, columns):
        return [
            vmem((n1, n2, rows, columns), BF16), vmem((n1, n2, rows, columns), BF16),
            vmem((n2, rows, columns), BF16), vmem((n2, rows, columns), BF16),
            sems(n1), sems(n1), sems(n2), sems(n2),
        ]

    plane_sum = 3 * two_step(nx, ny, hidden) + two_step(ny, nx, hidden)
    gather = [sems(n) for n in (ny, ny, ny, ny, nx, nx, nx, nx, nx, nx, ny, ny)]
    return pl.pallas_call(
        functools.partial(layer, ny, nx, nz, cap),
        out_shape=(
            jax.ShapeDtypeStruct((1, width // (ny * nx), hidden), F32),
            jax.ShapeDtypeStruct((1, rows, width), F32),
        ),
        in_specs=[any_spec] * 6 + [vmem_spec] * 2,
        out_specs=(vmem_spec, vmem_spec),
        scratch_shapes=[
            vmem(tokens.shape, BF16), vmem(cotangent.shape, BF16),
            vmem(latent_down.shape, BF16), vmem(latent_up.shape, BF16),
            vmem((width, hidden), BF16), vmem((hidden, width), BF16), sems(6),
            vmem((2 * tok_dev, width), BF16), vmem((2 * tok_dev, width), BF16),
            vmem((tok_dev, width), BF16), vmem((tok_dev, width), BF16), sems(2), sems(2),
            vmem((experts, cap, width), BF16), vmem((experts, cap, width), BF16),
            vmem((experts, cap, width), BF16), vmem((experts, cap, width), BF16),
            sems(2, experts), sems(2, experts), sems(2, 2),
            vmem((ny, nx, 2 * rows, hidden), BF16), vmem((ny, nx, rows, width), BF16), sems(2), sems(2),
            vmem((experts * cap, hidden), BF16), vmem((experts * cap, hidden), BF16),
            vmem((1, rows, 2 * width), BF16), vmem((1, rows, 2 * width), BF16),
            pltpu.SemaphoreType.DMA, pltpu.SemaphoreType.DMA,
        ]
        + plane_sum
        + plane_sum
        + gather,
        compiler_params=pltpu.CompilerParams(
            collective_id=0, has_side_effects=True, vmem_limit_bytes=56 * 1024 * 1024
        ),
        cost_estimate=pl.CostEstimate(flops=4 * 10**9, bytes_accessed=13 * 10**6, transcendentals=0),
    )(tokens, cotangent, latent_down, latent_up, expert_up, expert_down, routes.T, combine.T)


def solution(mesh):
    return jax.shard_map(
        functools.partial(shards, NY, NX),
        mesh=mesh,
        in_specs=(
            P(("dp", "expert"), "tensor"),
            P(("dp", "expert"), "tensor"),
            P("tensor", None),
            P(None, "tensor"),
            P(("expert", "tensor"), None, None),
            P(("expert", "tensor"), None, None),
            P(("dp", "expert", "tensor"), None),
            P(("dp", "expert", "tensor"), None),
        ),
        out_specs=(P(("expert", "tensor"), "dp", None), P(("expert", "tensor"), "dp", None)),
        check_vma=False,
    )
```

```python
import functools

import jax
import jax.numpy as jnp
from jax import lax
from jax.experimental import pallas as pl
from jax.experimental.pallas import tpu as pltpu
from jax.sharding import PartitionSpec as P

F32 = jnp.float32
BF16 = jnp.bfloat16
MESH = pl.DeviceIdType.MESH
NY, NX = 8, 4


def remote(src, dst, send_sem, recv_sem, device):
    return pltpu.make_async_remote_copy(
        src_ref=src,
        dst_ref=dst,
        send_sem=send_sem,
        recv_sem=recv_sem,
        device_id=device,
        device_id_type=MESH,
    )


def dot(a, b, dims=((1,), (0,))):
    return lax.dot_general(a, b, (dims, ((), ())), preferred_element_type=F32)


class Direct:
    def __init__(self, source, landing, sems, me, n, device):
        send_sem, recv_sem = sems
        self.sent, self.recv = [], []
        for k in range(1, n):
            target = lax.rem(me + k, n)
            sender = lax.rem(me + n - k, n)
            copy = remote(
                source(target), landing(me, k), send_sem.at[k], recv_sem.at[k], device(target)
            )
            copy.start()
            self.sent.append(copy)
            here = landing(sender, k)
            self.recv.append(remote(here, here, send_sem.at[k], recv_sem.at[k], device(target)))

    def wait(self):
        for copy in self.recv:
            copy.wait_recv()


class Ring:
    def __init__(self, me, n, device):
        self.me, self.n, self.device = me, n, device


class TwoStepSum:
    def __init__(self, refs, first, second):
        self.chunk, self.land, self.next, self.got, send1, recv1, send2, recv2 = refs
        self.first, self.second = first, second
        self.sems1, self.sems2 = (send1, recv1), (send2, recv2)

    def start(self):
        r = self.first
        self.step1 = Direct(
            lambda t: self.chunk.at[t], lambda s, k: self.land.at[k], self.sems1, r.me, r.n, r.device
        )

    def turn(self):
        self.step1.wait()
        r = self.second

        def ready(target):
            total = self.chunk[self.first.me, target].astype(F32)
            for k in range(1, self.first.n):
                total = total + self.land[k, target].astype(F32)
            self.next[target] = total.astype(BF16)
            return self.next.at[target]

        self.step2 = Direct(ready, lambda s, k: self.got.at[k], self.sems2, r.me, r.n, r.device)
        ready(r.me)

    def total(self):
        self.step2.wait()
        total = self.next[self.second.me].astype(F32)
        for k in range(1, self.second.n):
            total = total + self.got[k].astype(F32)
        return total

    def sent(self):
        return self.step1.sent + self.step2.sent


class PlaneSum:
    def __init__(self, refs, xs, ys):
        n = len(refs) // 3
        self.down = TwoStepSum(refs[:n], xs, ys)
        self.up0 = TwoStepSum(refs[n : 2 * n], xs, ys)
        self.up1 = TwoStepSum(refs[2 * n :], ys, xs)

    def totals(self):
        down, up0, up1 = self.down.total(), self.up0.total(), self.up1.total()
        hidden = up0.shape[1]
        return jnp.concatenate([down, up1[:, hidden:]], axis=1), up0, up1[:, :hidden]

    def sent(self):
        return self.down.sent() + self.up0.sent() + self.up1.sent()


def layer(
    ny, nx, nz, cap,
    tok_hbm, cot_hbm, down_hbm, up_hbm, wup_hbm, wdn_hbm, routes_ref, combine_ref,
    gup_ref, gdn_ref,
    tok, cot, down, up, wup, wdn, load_sem,
    part_f, part_b, got_f, got_b, swap_send, swap_recv,
    out_lat, out_grad, in_lat, in_grad, a2a_send, a2a_recv, own_sem,
    wup2, wdn2, slice_send, slice_recv,
    act_ref, pre_grad_ref, far_out, far_in, far_send, far_recv,
    *more,
):
    group = lax.axis_index("dp")
    z = lax.axis_index("expert")
    core = lax.axis_index("tensor")
    other = 1 - core
    y, x = group // nx, lax.rem(group, nx)
    tok_dev = routes_ref.shape[1]
    width, hidden = wup.shape
    experts = 2 * nz
    far = nz // 2
    reach = nz // 4
    far_z = lax.rem(z + far, nz)

    xs = Ring(x, nx, lambda xx: {"dp": y * nx + xx})
    ys = Ring(y, ny, lambda yy: {"dp": yy * nx + x})

    def plane(j):
        return lax.rem(z + j + nz, nz)

    loads = [
        pltpu.make_async_copy(src, dst, load_sem.at[i])
        for i, (src, dst) in enumerate(
            [(tok_hbm, tok), (down_hbm, down), (cot_hbm, cot), (up_hbm, up), (wup_hbm.at[0], wup), (wdn_hbm.at[0], wdn)]
        )
    ]
    for load in loads:
        load.start()

    barrier = pltpu.get_barrier_semaphore()
    greeted = []

    def greet(device):
        greeted.append(device)
        pl.semaphore_signal(barrier, inc=1, device_id=device, device_id_type=MESH)

    greet({"tensor": other})
    for j in range(1, nz):
        for cc in range(2):
            greet({"expert": plane(j), "tensor": cc})
    for k in range(1, nx):
        greet(xs.device(lax.rem(x + k, nx)))
    for k in range(1, ny):
        greet(ys.device(lax.rem(y + k, ny)))

    step = min(256, width)
    loads[0].wait()
    loads[1].wait()
    for j in range(0, width, step):
        part_f[:, j : j + step] = dot(tok[...], down[:, j : j + step]).astype(BF16)
    pl.semaphore_wait(barrier, len(greeted))
    theirs = pl.ds(pl.multiple_of(other * tok_dev, tok_dev), tok_dev)
    mine = pl.ds(pl.multiple_of(core * tok_dev, tok_dev), tok_dev)
    swap_f = remote(part_f.at[theirs], got_f, swap_send.at[0], swap_recv.at[0], {"tensor": other})
    swap_f.start()

    up_rows, dn_rows = wup2.shape[2], wdn2.shape[2]
    slices = [
        remote(
            wup_hbm.at[0, pl.ds(pl.multiple_of(group * up_rows, up_rows), up_rows)],
            wup2.at[y, x], slice_send.at[0], slice_recv.at[0], {"expert": far_z},
        ),
        remote(
            wdn_hbm.at[0, pl.ds(pl.multiple_of(group * dn_rows, dn_rows), dn_rows)],
            wdn2.at[y, x], slice_send.at[1], slice_recv.at[1], {"expert": far_z},
        ),
    ]

    @pl.when(core == 0)
    def _():
        for copy in slices:
            copy.start()

    loads[2].wait()
    loads[3].wait()
    for j in range(0, width, step):
        part_b[:, j : j + step] = dot(cot[...], up[j : j + step, :], ((1,), (1,))).astype(BF16)
    swap_b = remote(part_b.at[theirs], got_b, swap_send.at[1], swap_recv.at[1], {"tensor": other})
    swap_b.start()

    before = (
        lax.broadcasted_iota(jnp.int32, (tok_dev, tok_dev), 0)
        < lax.broadcasted_iota(jnp.int32, (tok_dev, tok_dev), 1)
    ).astype(BF16)
    expert_id = lax.broadcasted_iota(jnp.int32, (experts, tok_dev), 0)
    slot_id = lax.broadcasted_iota(jnp.int32, (experts * cap, tok_dev), 0)
    taken = jnp.zeros((experts, 1), F32)
    table = jnp.zeros((experts * cap, tok_dev), F32)
    weight = jnp.zeros((experts * cap, 1), F32)
    for k in range(routes_ref.shape[0]):
        chosen = routes_ref[k : k + 1, :]
        named = (expert_id == chosen).astype(F32)
        count = dot(named.astype(BF16), before) + taken
        rank = jnp.sum(named * count, axis=0, keepdims=True)
        taken = taken + jnp.sum(named, axis=1, keepdims=True)
        here = slot_id == chosen * cap + rank.astype(jnp.int32)
        table = table + here.astype(F32)
        weight = weight + jnp.sum(
            jnp.where(here, combine_ref[k : k + 1, :], 0.0), axis=1, keepdims=True
        )
    table = table.astype(BF16)

    second = [(k, k - far) for k in range(nz) if reach < k < nz - reach]
    first = [(k, k if k <= reach else k - nz) for k in range(nz) if k <= reach or k >= nz - reach]
    second_blocks, first_blocks = 2 * len(second), 2 * len(first)

    def places(moves, start):
        low = min(j for _, j in moves)
        return sorted([(k, j, start + 2 * (j - low)) for k, j in moves], key=lambda m: -abs(m[1]))

    second, first = places(second, 0), places(first, second_blocks)
    single = sorted([(k, k, 2 * k) for k in range(nz)], key=lambda m: -min(m[0], nz - m[0]))
    buffers = ((out_lat, in_lat), (out_grad, in_grad))

    def send(which, k, j, base, to, stay):
        outgoing, incoming = buffers[which]
        block = outgoing.at[2 * lax.rem(z + k, nz) + to]
        if stay:
            return pltpu.make_async_copy(block, incoming.at[base + to], own_sem.at[which, 0 if k == 0 else 1])
        return remote(
            block,
            incoming.at[base + core],
            a2a_send.at[which, nz * to + k],
            a2a_recv.at[which, base + core],
            {"tensor": to} if j == 0 else {"expert": plane(j), "tensor": to},
        )

    sent = []

    def dispatch(which, moves, to):
        for k, j, base in moves:
            if j != 0:
                copy = send(which, k, j, base, to, False)
                copy.start()
                sent.append(copy)
                continue

            @pl.when(core == to)
            def _():
                send(which, k, j, base, to, True).start()

            @pl.when(core != to)
            def _():
                send(which, k, j, base, to, False).start()

    def collect(which, moves, me):
        incoming = buffers[which][1]
        for k, j, base in reversed(moves):
            for source in range(2):
                if j == 0 and source == me:
                    send(which, k, j, base, me, True).wait()
                    continue
                here = incoming.at[base + source]
                remote(
                    here, here, a2a_send.at[which, k], a2a_recv.at[which, base + source], {"tensor": other}
                ).wait_recv()

    swap_f.wait_recv()
    lat = (part_f[mine].astype(F32) + got_f[...].astype(F32)).astype(BF16)
    out_lat[...] = dot(table, lat).astype(BF16).reshape(out_lat.shape)
    dispatch(0, first, 0)
    swap_b.wait_recv()
    back = dot(table, part_b[mine]) + dot(table, got_b[...])
    out_grad[...] = (weight * back).astype(BF16).reshape(out_grad.shape)
    dispatch(1, first, 0)
    dispatch(0, second, 0)
    dispatch(1, second, 0)
    dispatch(0, single, 1)
    dispatch(1, single, 1)

    per_sum = len(SUM_PARTS) * 8
    sums = [PlaneSum(more[i * per_sum : (i + 1) * per_sum], xs, ys) for i in range(2)]
    gather = more[2 * per_sum :]

    def expert(moves, me, start, blocks, weight_up, weight_down, summed):
        block = pl.ds(start, blocks)
        rows = pl.ds(start * cap, blocks * cap)
        collect(0, moves, me)
        lat_rows = in_lat[block].reshape(-1, width)
        positive = jnp.maximum(dot(lat_rows, weight_up), 0.0)
        act_ref[rows] = (positive * positive).astype(BF16)
        collect(1, moves, me)
        grad_rows = in_grad[block].reshape(-1, width)
        hidden_grad = dot(grad_rows, weight_down, ((1,), (1,)))
        pre_grad_ref[rows] = (hidden_grad * 2.0 * positive).astype(BF16)
        main = width - width // 8
        for j in range(0, width, step):
            piece = dot(act_ref[rows], grad_rows[:, j : j + step], ((0,), (0,)))
            piece = piece.astype(BF16).reshape(ny, nx, dn_rows, step)
            stop = min(j + step, main)
            for xx in range(nx):
                summed.down.chunk[xx, :, :, j:stop] = piece[:, xx, :, : stop - j]
            if stop < j + step:
                summed.up1.chunk[:, :, :, hidden + stop - main : hidden + j + step - main] = piece[..., stop - j :]
        summed.down.start()
        cut = min(step, hidden)
        for j in range(0, hidden, cut):
            piece = dot(lat_rows, pre_grad_ref[rows, j : j + cut], ((0,), (0,)))
            piece = piece.astype(BF16).reshape(ny, nx, 2, dn_rows, cut)
            for xx in range(nx):
                summed.up0.chunk[xx, :, :, j : j + cut] = piece[:, xx, 0]
            summed.up1.chunk[:, :, :, j : j + cut] = piece[:, :, 1]
        summed.up1.start()
        summed.up0.start()

    def finish(down_sum, up0_sum, up1_sum):
        gdn_ref[0] = down_sum
        gup_ref[0, 0:dn_rows, :] = up0_sum
        gup_ref[0, dn_rows : 2 * dn_rows, :] = up1_sum

    def sent_within(to, moves):
        for k, j, base in moves:
            if j == 0:
                for which in range(2):
                    send(which, k, j, base, to, False).wait_send()

    @pl.when(core == 0)
    def _():
        up0, up1 = pl.ds(0, dn_rows), pl.ds(dn_rows, dn_rows)
        g = [gather[2 * i : 2 * i + 2] for i in range(6)]
        for copy in slices:
            copy.wait_recv()
        a1 = Direct(lambda t: wdn2.at[y, x], lambda s, k: wdn2.at[s, x], g[0], y, ny, ys.device)
        b1 = Direct(lambda t: wup2.at[y, x, up1], lambda s, k: wup2.at[y, s, up1], g[2], x, nx, xs.device)
        c1 = Direct(lambda t: wup2.at[y, x, up0], lambda s, k: wup2.at[s, x, up0], g[1], y, ny, ys.device)
        b1.wait()
        b2 = Direct(lambda t: wup2.at[y, :, up1], lambda s, k: wup2.at[s, :, up1], g[5], y, ny, ys.device)
        a1.wait()
        a2 = Direct(lambda t: wdn2.at[:, x], lambda s, k: wdn2.at[:, s], g[3], x, nx, xs.device)
        c1.wait()
        c2 = Direct(lambda t: wup2.at[:, x, up0], lambda s, k: wup2.at[:, s, up0], g[4], x, nx, xs.device)

        home, away = sums
        loads[4].wait()
        loads[5].wait()
        expert(first, 0, second_blocks, first_blocks, wup[...], wdn[...], home)
        for part in (a2, b2, c2):
            part.wait()
        expert(
            second, 0, 0, second_blocks,
            wup2[...].reshape(width, hidden), wdn2[...].reshape(hidden, width), away,
        )
        for summed in (home, away):
            summed.down.turn()
            summed.up1.turn()
            summed.up0.turn()
        down_sum, up0_sum, up1_sum = away.totals()
        far_out[0, :, :width] = down_sum.astype(BF16)
        far_out[0, :, width : width + hidden] = up0_sum.astype(BF16)
        far_out[0, :, width + hidden :] = up1_sum.astype(BF16)
        back_home = remote(far_out, far_in, far_send, far_recv, {"expert": far_z})
        back_home.start()
        totals = home.totals()
        back_home.wait_recv()
        finish(
            totals[0] + far_in[0, :, :width].astype(F32),
            totals[1] + far_in[0, :, width : width + hidden].astype(F32),
            totals[2] + far_in[0, :, width + hidden :].astype(F32),
        )
        sent_within(1, single)
        for copy in slices + [back_home] + home.sent() + away.sent():
            copy.wait_send()
        for part in (a1, b1, c1, a2, b2, c2):
            for copy in part.sent:
                copy.wait_send()

    @pl.when(core == 1)
    def _():
        loads[4].wait()
        loads[5].wait()
        summed = sums[0]
        expert(single, 1, 0, 2 * nz, wup[...], wdn[...], summed)
        summed.down.turn()
        summed.up1.turn()
        summed.up0.turn()
        finish(*summed.totals())
        sent_within(0, first + second)
        for copy in summed.sent():
            copy.wait_send()

    for copy in [swap_f, swap_b] + sent:
        copy.wait_send()


SUM_PARTS = ("down", "up0", "up1")


def shards(ny, nx, tokens, cotangent, latent_down, latent_up, expert_up, expert_down, routes, combine):
    nz = lax.axis_size("expert")
    tok_dev, top = routes.shape
    width, hidden = expert_up.shape[1:]
    experts = 2 * nz
    cap = max(2, 3 * tok_dev * top // (2 * experts))
    rows = hidden // (ny * nx)
    assert width == 2 * hidden

    def sems(*shape):
        return pltpu.SemaphoreType.DMA(shape)

    vmem = pltpu.VMEM
    any_spec = pl.BlockSpec(memory_space=pl.ANY)
    vmem_spec = pl.BlockSpec(memory_space=pltpu.VMEM)

    def two_step(n1, n2, columns):
        return [
            vmem((n1, n2, rows, columns), BF16), vmem((n1, n2, rows, columns), BF16),
            vmem((n2, rows, columns), BF16), vmem((n2, rows, columns), BF16),
            sems(n1), sems(n1), sems(n2), sems(n2),
        ]

    plane_sum = (
        two_step(nx, ny, width - width // 8)
        + two_step(nx, ny, hidden)
        + two_step(ny, nx, hidden + width // 8)
    )
    gather = [sems(n) for n in (ny, ny, ny, ny, nx, nx, nx, nx, nx, nx, ny, ny)]
    return pl.pallas_call(
        functools.partial(layer, ny, nx, nz, cap),
        out_shape=(
            jax.ShapeDtypeStruct((1, width // (ny * nx), hidden), F32),
            jax.ShapeDtypeStruct((1, rows, width), F32),
        ),
        in_specs=[any_spec] * 6 + [vmem_spec] * 2,
        out_specs=(vmem_spec, vmem_spec),
        scratch_shapes=[
            vmem(tokens.shape, BF16), vmem(cotangent.shape, BF16),
            vmem(latent_down.shape, BF16), vmem(latent_up.shape, BF16),
            vmem((width, hidden), BF16), vmem((hidden, width), BF16), sems(6),
            vmem((2 * tok_dev, width), BF16), vmem((2 * tok_dev, width), BF16),
            vmem((tok_dev, width), BF16), vmem((tok_dev, width), BF16), sems(2), sems(2),
            vmem((experts, cap, width), BF16), vmem((experts, cap, width), BF16),
            vmem((experts, cap, width), BF16), vmem((experts, cap, width), BF16),
            sems(2, experts), sems(2, experts), sems(2, 2),
            vmem((ny, nx, 2 * rows, hidden), BF16), vmem((ny, nx, rows, width), BF16), sems(2), sems(2),
            vmem((experts * cap, hidden), BF16), vmem((experts * cap, hidden), BF16),
            vmem((1, rows, 2 * width), BF16), vmem((1, rows, 2 * width), BF16),
            pltpu.SemaphoreType.DMA, pltpu.SemaphoreType.DMA,
        ]
        + plane_sum
        + plane_sum
        + gather,
        compiler_params=pltpu.CompilerParams(
            collective_id=0, has_side_effects=True, vmem_limit_bytes=56 * 1024 * 1024
        ),
        cost_estimate=pl.CostEstimate(flops=4 * 10**9, bytes_accessed=13 * 10**6, transcendentals=0),
    )(tokens, cotangent, latent_down, latent_up, expert_up, expert_down, routes.T, combine.T)


def solution(mesh):
    return jax.shard_map(
        functools.partial(shards, NY, NX),
        mesh=mesh,
        in_specs=(
            P(("dp", "expert"), "tensor"),
            P(("dp", "expert"), "tensor"),
            P("tensor", None),
            P(None, "tensor"),
            P(("expert", "tensor"), None, None),
            P(("expert", "tensor"), None, None),
            P(("dp", "expert", "tensor"), None),
            P(("dp", "expert", "tensor"), None),
        ),
        out_specs=(P(("expert", "tensor"), "dp", None), P(("expert", "tensor"), "dp", None)),
        check_vma=False,
    )
```
